512 devices in a mesh: space: 64 (over z_lo, x, core), batch: 8 (over z_hi, y).
Axes of the slice: x: 4, y: 4, z: 16 (z_hi: 2, z_lo: 8; z = z_hi * 8 + z_lo), core: 2. Of those that a mesh axis runs over, the one named last changes fastest.
Arguments:
- fine_parts: bfloat16 [8, 32768, 128], P('batch', 'space'), may hold values from -5 to 5
- parent_parts: bfloat16 [8, 4096, 128], P('batch', 'space'), may hold values from -5 to 5
- coarse_local: float32 [4096, 128], P('space'), may hold values from -6 to 6
- fine_source: int32 [189, 32768], P(None, 'space'), may hold values from 0 to 159
- fine_operator: int32 [189, 32768], P(None, 'space'), may hold values from 0 to 63
- parent_source: int32 [189, 4096], P(None, 'space'), may hold values from 0 to 159
- parent_operator: int32 [189, 4096], P(None, 'space'), may hold values from 0 to 63
- operators: bfloat16 [64, 128, 128], replicated, may hold values from -0.0390625 to 0.0390625
- child_shift: bfloat16 [8, 128, 128], replicated, may hold values from -0.5 to 0.5
- basis: bfloat16 [32768, 128, 128], P('space', 'batch'), may hold values from -0.5 to 0.5
- counts: int32 [8, 32768], P('batch', 'space'), may hold values from 1 to 16
Outputs:
- potential: float32 [128, 32768], P('batch', 'space')
The draws below stay inside these ranges and needn't reach their ends.
Inputs may be any that keep to these rules, and one draw needn't show every extreme that they name: `fine_source`: an entry v names, in the target's own block if v // 32 is 0 and else in the block whose index differs from the target's in bit v // 32 - 1, box v % 32 of the aligned group of 32 boxes that holds the target's position. `parent_source`: an entry v names, in the target's own block if v // 32 is 0 and else in the block whose index differs from the target's in bit v // 32 - 1, parent box v % 32 of the aligned group of 32 parent boxes that holds the target's position.
All inputs are finite; a program needn't handle non-finite values.
Results may differ from the reference program's by a relative error of at most 0.015.
Values may be sent and summed in bfloat16 or wider, within the bound.
A program may use at most 64 MiB of HBM per device.

```python
import math
import jax
import jax.numpy as jnp
from jax import lax

NC = 128
NTERMS = 121
NI = 189
NOPS = 64
BOX_DEV = 512
SLOT_DEV = 16
PB_DEV = 64
WINDOW = 32
NBATCH = 8
NBOX = 32768
PNBOX = 4096
SLOTS = 128


def with_ends(drawn, own_key, low, high):
    extent = drawn.shape
    place = [jax.random.randint(jax.random.fold_in(own_key, axis), (), 0, extent[axis]) for axis in range(len(extent))]
    drawn = drawn.at[tuple(place)].set(low)
    longest = extent.index(max(extent))
    place[longest] = (place[longest] + 1) % extent[longest]
    return drawn.at[tuple(place)].set(high)


def level_of(own_key, shape, split, low, high):
    loudness = 1.0
    for position, shards_of in split:
        heights = jax.random.uniform(jax.random.fold_in(jax.random.fold_in(own_key, 6), position), (shards_of,), jnp.float32, low / len(split), high / len(split))
        loudness = loudness * jnp.repeat(jnp.exp(heights), shape[position] // shards_of).reshape((-1,) + (1,) * (len(shape) - 1 - position))
    return loudness


def centred(stream_key, shape, scale, limit, split=(), kind=jnp.bfloat16):
    entries = scale * jax.random.normal(stream_key, shape, jnp.float32)
    if split:
        entries = entries * level_of(stream_key, shape, split, -0.22, 0.18)
    return jnp.clip(entries, -limit, limit).astype(kind)


def setup_inputs(seed: int = 0) -> dict:
    streams_of = jax.random.split(jax.random.key(seed), 12)
    return {
        "fine_parts": centred(streams_of[0], (NBATCH, NBOX, NC), (1.0 / NBATCH ** 0.5), 5.0, ((0, 8), (1, 64))),
        "parent_parts": centred(streams_of[1], (NBATCH, PNBOX, NC), (1.0 / NBATCH ** 0.5), 5.0, ((0, 8), (1, 64))),
        "coarse_local": centred(streams_of[2], (PNBOX, NC), 1.0, 6.0, ((0, 64),), jnp.float32),
        "fine_source": with_ends(jax.random.randint(streams_of[3], (NI, NBOX), 0, 5 * WINDOW), jax.random.fold_in(streams_of[3], 1), 0, (5 * WINDOW) - 1).astype(jnp.int32),
        "fine_operator": with_ends(jax.random.randint(streams_of[4], (NI, NBOX), 0, NOPS), jax.random.fold_in(streams_of[4], 1), 0, NOPS - 1).astype(jnp.int32),
        "parent_source": with_ends(jax.random.randint(streams_of[5], (NI, PNBOX), 0, 5 * WINDOW), jax.random.fold_in(streams_of[5], 1), 0, (5 * WINDOW) - 1).astype(jnp.int32),
        "parent_operator": with_ends(jax.random.randint(streams_of[6], (NI, PNBOX), 0, NOPS), jax.random.fold_in(streams_of[6], 1), 0, NOPS - 1).astype(jnp.int32),
        "operators": centred(streams_of[7], (NOPS, NC, NC), (NC * NI) ** -0.5, 0.0390625),
        "child_shift": centred(streams_of[8], (8, NC, NC), NC ** -0.5, 0.5),
        "basis": centred(streams_of[9], (NBOX, SLOTS, NC), NTERMS ** -0.5, 0.5, ((0, 64), (1, 8))),
        "counts": with_ends(jax.random.randint(streams_of[10], (NBATCH, NBOX), 1, SLOT_DEV + 1), jax.random.fold_in(streams_of[10], 1), 1, SLOT_DEV).astype(jnp.int32),
    }


def far_field(multipole, source_list, operator_list, block_rows, operators):
    total_rows, coef_width = multipole.shape
    kind_count = operators.shape[0]
    list_length = source_list.shape[0]
    box_index = jnp.arange(total_rows, dtype=jnp.int32)
    owner_block = (box_index // block_rows)[None, :]
    group_start = ((box_index % block_rows) // WINDOW * WINDOW)[None, :]
    which_block = source_list // WINDOW
    flipped = jnp.bitwise_xor(owner_block, jnp.left_shift(jnp.ones_like(which_block), jnp.maximum(which_block - 1, 0)))
    home_block = jnp.where(which_block == 0, owner_block, flipped)
    global_source = (home_block * block_rows + group_start + source_list % WINDOW).astype(jnp.int32)
    flat_ops = operators.reshape(kind_count * coef_width, coef_width)
    piece_rows = math.gcd(total_rows, 256)
    piece_count = total_rows // piece_rows
    source_pieces = global_source.reshape(list_length, piece_count, piece_rows).transpose(1, 0, 2)
    kind_pieces = operator_list.reshape(list_length, piece_count, piece_rows).transpose(1, 0, 2)
    kinds_iota = jnp.arange(kind_count, dtype=jnp.int32)

    def one_piece(pieces):
        sources, kinds = pieces
        gathered = multipole[sources].astype(jnp.float32)
        onehot = (kinds[:, :, None] == kinds_iota).astype(jnp.float32)
        grouped = jnp.einsum("jbt,jbk->btk", onehot, gathered).astype(jnp.bfloat16)
        return jnp.dot(grouped.reshape(piece_rows, kind_count * coef_width), flat_ops, preferred_element_type=jnp.float32)

    return lax.map(one_piece, (source_pieces, kind_pieces)).reshape(total_rows, coef_width)


def reference(fine_parts, parent_parts, coarse_local, fine_source, fine_operator, parent_source, parent_operator, operators, child_shift, basis, counts):
    fine_mult = jnp.sum(fine_parts.astype(jnp.float32), axis=0).astype(jnp.bfloat16)
    parent_mult = jnp.sum(parent_parts.astype(jnp.float32), axis=0).astype(jnp.bfloat16)
    fine_far = far_field(fine_mult, fine_source, fine_operator, BOX_DEV, operators)
    parent_far = far_field(parent_mult, parent_source, parent_operator, PB_DEV, operators)
    parent_local = (coarse_local + parent_far).astype(jnp.bfloat16)
    shifted = jnp.einsum("pk,okl->pol", parent_local.astype(jnp.float32), child_shift.astype(jnp.float32)).reshape(fine_far.shape)
    coef_width = fine_far.shape[1]
    keep = jnp.arange(coef_width, dtype=jnp.int32) < NTERMS
    local = jnp.where(keep[None, :], shifted + fine_far, 0.0).astype(jnp.bfloat16)
    total_rows = local.shape[0]
    piece_rows = math.gcd(total_rows, 256)
    piece_count = total_rows // piece_rows
    basis_pieces = basis.reshape(piece_count, piece_rows, basis.shape[1], basis.shape[2])
    local_pieces = local.reshape(piece_count, piece_rows, coef_width)

    def evaluate(pieces):
        block_basis, block_local = pieces
        return jnp.einsum("bsk,bk->bs", block_basis.astype(jnp.float32), block_local.astype(jnp.float32))

    values = lax.map(evaluate, (basis_pieces, local_pieces)).reshape(total_rows, basis.shape[1]).T
    slot_index = jnp.arange(values.shape[0], dtype=jnp.int32)[:, None] % SLOT_DEV
    limits = jnp.repeat(counts, SLOT_DEV, axis=0)
    return jnp.where(slot_index < limits, values, 0.0)
```

```python
import functools

import jax
import jax.numpy as jnp
from jax import lax
from jax.experimental import pallas as pl
from jax.experimental.pallas import tpu as pltpu
from jax.sharding import PartitionSpec as P

NTERMS = 121
NI = 189
NC = 128
NOPS = 64
WINDOW = 32
REACH = 5 * WINDOW
ROWS = 128
PROWS = 16
WINDOWS = ROWS // WINDOW
MESH = pl.DeviceIdType.MESH
F32 = jnp.float32
BF16 = jnp.bfloat16


def remote(src, dst, send_sem, recv_sem, device):
    return pltpu.make_async_remote_copy(
        src_ref=src,
        dst_ref=dst,
        send_sem=send_sem,
        recv_sem=recv_sem,
        device_id=device,
        device_id_type=MESH,
    )


def greet(devices):
    barrier = pltpu.get_barrier_semaphore()
    for device in devices:
        pl.semaphore_signal(barrier, inc=1, device_id=device, device_id_type=MESH)


def await_greetings(devices):
    pl.semaphore_wait(pltpu.get_barrier_semaphore(), len(devices))


def one_box(source_row, kind_row, iota_ref):
    source = jnp.broadcast_to(source_row, (16, 256)).astype(BF16)
    kind = jnp.broadcast_to(kind_row, (16, 256)).astype(BF16)
    one, none = jnp.ones((), BF16), jnp.zeros((), BF16)
    iota = iota_ref[...]
    sources = jnp.concatenate([source] * (REACH // 16), axis=0)
    kinds = jnp.concatenate([kind] * (NOPS // 16), axis=0)
    chosen = jnp.where(sources == iota, one, none)
    onehot = jnp.where(kinds == iota[:NOPS], one, none)
    counted = lax.dot_general(
        onehot, chosen, (((1,), (1,)), ((), ())), preferred_element_type=F32
    )
    return jnp.concatenate([counted, jnp.zeros((NOPS, 256 - REACH), F32)], axis=1)


def lists_across(source_v, kind_v):
    entry = lax.broadcasted_iota(jnp.int32, (256, 1), 0)
    source = jnp.where(entry < NI, source_v[...], 255).astype(F32)
    kind = jnp.where(entry < NI, kind_v[...], 255).astype(F32)
    return source.T, kind.T


def kernel(
    fine_parts,
    parent_parts,
    coarse,
    fine_source,
    fine_operator,
    parent_source,
    parent_operator,
    operators,
    child_shift,
    basis,
    out,
    source_v,
    kind_v,
    psource_v,
    pkind_v,
    source_t,
    kind_t,
    psource_t,
    pkind_t,
    iota_v,
    own_v,
    coarse_v,
    ops_v,
    shift_v,
    basis_v,
    counted_f,
    counted_v,
    pcounted_v,
    from_y,
    half_v,
    from_z,
    near_v,
    grouped_v,
    spread_v,
    local_v,
    load_sem,
    y_send,
    y_recv,
    z_send,
    z_recv,
    n_send,
    n_recv,
    l_send,
    l_recv,
):
    d = lax.axis_index("space")
    i = lax.axis_index("batch")
    h, y = i // 4, i % 4
    y_peers = [(d, h * 4 + (y + o) % 4) for o in (1, 2, 3)]
    z_peer = (d, (1 - h) * 4 + y)
    partners = [(d + (1 - 2 * ((d // s) % 2)) * s, i) for s in (1, 2, 4, 8)]
    everyone = y_peers + [z_peer] + partners
    greet(everyone)

    def load(src, dst, n):
        copy = pltpu.make_async_copy(src, dst, load_sem.at[n])
        copy.start()
        return copy

    row0 = pl.multiple_of(y * ROWS, ROWS)
    prow0 = pl.multiple_of(y * PROWS, PROWS)
    pwin0 = pl.multiple_of((y // 2) * WINDOW, WINDOW)
    lists = [
        load(parent_source, psource_v.at[pl.ds(0, NI)], 0),
        load(parent_operator, pkind_v.at[pl.ds(0, NI)], 1),
        load(fine_source.at[:, pl.ds(row0, ROWS)], source_v.at[pl.ds(0, NI)], 2),
        load(fine_operator.at[:, pl.ds(row0, ROWS)], kind_v.at[pl.ds(0, NI)], 3),
    ]
    mine = [
        load(fine_parts.at[0, pl.ds(row0, ROWS)], own_v.at[pl.ds(0, ROWS)], 4),
        load(parent_parts.at[0, pl.ds(pwin0, WINDOW)], own_v.at[pl.ds(ROWS, WINDOW)], 5),
        load(coarse.at[pl.ds(prow0, PROWS)], coarse_v, 6),
    ]
    weights = [
        load(operators, ops_v, 7),
        load(child_shift, shift_v, 8),
        load(basis, basis_v, 9),
    ]

    iota_v[...] = lax.broadcasted_iota(jnp.int32, (REACH, 256), 0).astype(F32).astype(BF16)
    for copy in lists:
        copy.wait()
    psource_t[...], pkind_t[...] = lists_across(psource_v, pkind_v)
    source_t[...], kind_t[...] = lists_across(source_v, kind_v)

    def count_into(source_ref, kind_ref, start, boxes, target):
        def few(step, carry):
            for k in range(4):
                b = step * 4 + k
                counted = one_box(
                    source_ref[pl.ds(start + b, 1), :], kind_ref[pl.ds(start + b, 1), :], iota_v
                )
                counted_f[0, pl.ds(b, NOPS, stride=boxes), :] = counted[:, :128]
                counted_f[1, pl.ds(b, NOPS, stride=boxes), :] = counted[:, 128:]
            return carry

        lax.fori_loop(0, boxes // 4, few, 0)

        def narrow(step, carry):
            rows = pl.ds(pl.multiple_of(step * 256, 256), 256)
            target[rows, 0:128] = counted_f[0, rows, :].astype(BF16)
            target[rows, 128:256] = counted_f[1, rows, :].astype(BF16)
            return carry

        lax.fori_loop(0, NOPS * boxes // 256, narrow, 0)

    def count_windows(first, last):
        def window(w, carry):
            count_into(source_t, kind_t, w * WINDOW, WINDOW, counted_v.at[w])
            return carry

        lax.fori_loop(first, last, window, 0)

    count_into(psource_t, pkind_t, prow0, PROWS, pcounted_v)

    await_greetings(everyone)
    sends = []
    y_copies = []
    for o, device in enumerate(y_peers):
        there = (y + o + 1) % 4
        theirs = pl.multiple_of(there * ROWS, ROWS)
        theirs_p = pl.multiple_of((there // 2) * WINDOW, WINDOW)
        y_copies.append(
            remote(
                fine_parts.at[0, pl.ds(theirs, ROWS)],
                from_y.at[o, pl.ds(0, ROWS)],
                y_send.at[2 * o],
                y_recv.at[2 * o],
                device,
            )
        )
        y_copies.append(
            remote(
                parent_parts.at[0, pl.ds(theirs_p, WINDOW)],
                from_y.at[o, pl.ds(ROWS, WINDOW)],
                y_send.at[2 * o + 1],
                y_recv.at[2 * o + 1],
                device,
            )
        )
    for copy in y_copies:
        copy.start()
    sends += y_copies

    count_windows(0, 1)
    for copy in mine:
        copy.wait()
    for copy in y_copies:
        copy.wait_recv()
    half = own_v[...].astype(F32)
    for o in range(3):
        half = half + from_y[o].astype(F32)
    half_v[...] = half.astype(BF16)

    z_copy = remote(half_v, from_z, z_send, z_recv, z_peer)
    z_copy.start()
    sends.append(z_copy)
    count_windows(1, 3)
    z_copy.wait_recv()
    near_v[0] = (half_v[...].astype(F32) + from_z[...].astype(F32)).astype(BF16)

    n_copies = [
        remote(near_v.at[0], near_v.at[k + 1], n_send.at[k], n_recv.at[k], device)
        for k, device in enumerate(partners)
    ]
    for copy in n_copies:
        copy.start()
    sends += n_copies
    count_windows(3, 4)
    for copy in weights:
        copy.wait()
    for copy in n_copies:
        copy.wait_recv()

    nothing = jnp.zeros((256 - REACH, NC), BF16)
    for w in range(WINDOWS + 1):
        fine = w < WINDOWS
        boxes = WINDOW if fine else PROWS
        near = near_v[:, w * WINDOW : (w + 1) * WINDOW, :].reshape(REACH, NC)
        near = jnp.concatenate([near, nothing], axis=0)
        counted = counted_v.at[w] if fine else pcounted_v
        kinds = 512 // boxes
        for c in range(NOPS // kinds):
            grouped = jnp.dot(
                counted[c * 512 : (c + 1) * 512, :], near, preferred_element_type=F32
            ).astype(BF16)
            for t in range(kinds):
                kind = c * kinds + t
                grouped_v[
                    w * WINDOW : w * WINDOW + boxes, kind * NC : (kind + 1) * NC
                ] = grouped[t * boxes : (t + 1) * boxes, :]
    far = jnp.dot(
        grouped_v[...], ops_v[...].reshape(NOPS * NC, NC), preferred_element_type=F32
    )
    parent_local = (coarse_v[...] + far[ROWS:, :]).astype(BF16)
    for octant in range(8):
        spread_v[pl.ds(octant, PROWS, stride=8), :] = jnp.dot(
            parent_local, shift_v[octant], preferred_element_type=F32
        )
    keep = lax.broadcasted_iota(jnp.int32, (ROWS, NC), 1) < NTERMS
    local_v[pl.ds(row0, ROWS), :] = jnp.where(keep, spread_v[...] + far[:ROWS, :], 0.0).astype(BF16)

    l_copies = [
        remote(
            local_v.at[pl.ds(row0, ROWS)],
            local_v.at[pl.ds(row0, ROWS)],
            l_send.at[o],
            l_recv.at[o],
            device,
        )
        for o, device in enumerate(y_peers)
    ]
    for copy in l_copies:
        copy.start()
    sends += l_copies

    lane = lax.broadcasted_iota(jnp.int32, (16, ROWS), 1)

    def evaluate(start):
        local = local_v[pl.ds(start, ROWS), :]
        found = jnp.zeros((16, ROWS), F32)
        for c in range(ROWS // 32):
            slots = basis_v[pl.ds(start + c * 32, 32)].reshape(32 * 16, NC)
            values = lax.dot_general(
                slots, local, (((1,), (1,)), ((), ())), preferred_element_type=F32
            )
            for b in range(32):
                found = jnp.where(lane == c * 32 + b, values[b * 16 : (b + 1) * 16, :], found)
        out[:, pl.ds(start, ROWS)] = found

    evaluate(row0)
    for o, copy in enumerate(l_copies):
        copy.wait_recv()
        evaluate(pl.multiple_of(((y + 3 - o) % 4) * ROWS, ROWS))
    for copy in sends:
        copy.wait_send()


def body(
    fine_parts,
    parent_parts,
    coarse_local,
    fine_source,
    fine_operator,
    parent_source,
    parent_operator,
    operators,
    child_shift,
    basis,
    counts,
):
    boxes, slots, _ = basis.shape
    parents = coarse_local.shape[0]
    vmem = pltpu.VMEM
    dma = pltpu.SemaphoreType.DMA
    message = ROWS + WINDOW
    values = pl.pallas_call(
        kernel,
        out_shape=jax.ShapeDtypeStruct((slots, boxes), F32),
        in_specs=[pl.BlockSpec(memory_space=pl.ANY)] * 10,
        out_specs=pl.BlockSpec(memory_space=pltpu.VMEM),
        scratch_shapes=[
            vmem((256, ROWS), jnp.int32),
            vmem((256, ROWS), jnp.int32),
            vmem((256, parents), jnp.int32),
            vmem((256, parents), jnp.int32),
            vmem((ROWS, 256), F32),
            vmem((ROWS, 256), F32),
            vmem((parents, 256), F32),
            vmem((parents, 256), F32),
            vmem((REACH, 256), BF16),
            vmem((message, NC), BF16),
            vmem((PROWS, NC), F32),
            vmem((NOPS, NC, NC), BF16),
            vmem((8, NC, NC), BF16),
            vmem((boxes, slots, NC), BF16),
            vmem((2, NOPS * WINDOW, 128), F32),
            vmem((WINDOWS, NOPS * WINDOW, 256), BF16),
            vmem((NOPS * PROWS, 256), BF16),
            vmem((3, message, NC), BF16),
            vmem((message, NC), BF16),
            vmem((message, NC), BF16),
            vmem((5, message, NC), BF16),
            vmem((ROWS + PROWS, NOPS * NC), BF16),
            vmem((ROWS, NC), F32),
            vmem((boxes, NC), BF16),
            dma((10,)),
            dma((6,)),
            dma((6,)),
            dma,
            dma,
            dma((4,)),
            dma((4,)),
            dma((3,)),
            dma((3,)),
        ],
        compiler_params=pltpu.CompilerParams(
            collective_id=0, has_side_effects=True, vmem_limit_bytes=40 * 1024 * 1024
        ),
    )(
        fine_parts,
        parent_parts,
        coarse_local,
        fine_source,
        fine_operator,
        parent_source,
        parent_operator,
        operators,
        child_shift,
        basis,
    )
    slot_index = lax.iota(jnp.int32, slots)[:, None]
    return jnp.where(slot_index < counts, values, 0.0)


def solution(mesh):
    placed = (
        P("batch", "space", None),
        P("batch", "space", None),
        P("space", None),
        P(None, "space"),
        P(None, "space"),
        P(None, "space"),
        P(None, "space"),
        P(),
        P(),
        P("space", "batch", None),
        P("batch", "space"),
    )
    return jax.shard_map(
        body, mesh=mesh, in_specs=placed, out_specs=P("batch", "space"), check_vma=False
    )
```

```python
import functools

import jax
import jax.numpy as jnp
from jax import lax
from jax.experimental import pallas as pl
from jax.experimental.pallas import tpu as pltpu
from jax.sharding import PartitionSpec as P

NTERMS = 121
NI = 189
NC = 128
NOPS = 64
WINDOW = 32
REACH = 5 * WINDOW
ROWS = 128
PROWS = 16
WINDOWS = ROWS // WINDOW
MESSAGE = WINDOW + ROWS
FIRST = 3 * WINDOW
PIECES = ((slice(0, FIRST), (0, 1)), (slice(FIRST, MESSAGE), (2,)))
MESH = pl.DeviceIdType.MESH
F32 = jnp.float32
BF16 = jnp.bfloat16


def remote(src, dst, send_sem, recv_sem, device):
    return pltpu.make_async_remote_copy(
        src_ref=src,
        dst_ref=dst,
        send_sem=send_sem,
        recv_sem=recv_sem,
        device_id=device,
        device_id_type=MESH,
    )


def greet(devices):
    barrier = pltpu.get_barrier_semaphore()
    for device in devices:
        pl.semaphore_signal(barrier, inc=1, device_id=device, device_id_type=MESH)


def await_greetings(devices):
    pl.semaphore_wait(pltpu.get_barrier_semaphore(), len(devices))


def one_box(source_row, kind_row, iota_ref):
    source = jnp.broadcast_to(source_row, (16, 256)).astype(BF16)
    kind = jnp.broadcast_to(kind_row, (16, 256)).astype(BF16)
    one, none = jnp.ones((), BF16), jnp.zeros((), BF16)
    iota = iota_ref[...]
    sources = jnp.concatenate([source] * (REACH // 16), axis=0)
    kinds = jnp.concatenate([kind] * (NOPS // 16), axis=0)
    chosen = jnp.where(sources == iota, one, none)
    onehot = jnp.where(kinds == iota[:NOPS], one, none)
    counted = lax.dot_general(
        onehot, chosen, (((1,), (1,)), ((), ())), preferred_element_type=F32
    )
    return jnp.concatenate([counted, jnp.zeros((NOPS, 256 - REACH), F32)], axis=1)


def lists_across(source_v, kind_v):
    entry = lax.broadcasted_iota(jnp.int32, (256, 1), 0)
    source = jnp.where(entry < NI, source_v[...], 255).astype(F32)
    kind = jnp.where(entry < NI, kind_v[...], 255).astype(F32)
    return source.T, kind.T


def kernel(
    fine_parts,
    parent_parts,
    coarse,
    fine_source,
    fine_operator,
    parent_source,
    parent_operator,
    operators,
    child_shift,
    basis,
    out,
    source_v,
    kind_v,
    psource_v,
    pkind_v,
    source_t,
    kind_t,
    psource_t,
    pkind_t,
    iota_v,
    own_v,
    coarse_v,
    ops_v,
    shift_v,
    basis_v,
    counted_f,
    counted_v,
    pcounted_v,
    from_y,
    half_v,
    from_z,
    near_v,
    grouped_v,
    spread_v,
    local_v,
    load_sem,
    y_send,
    y_recv,
    z_send,
    z_recv,
    n_send,
    n_recv,
    l_send,
    l_recv,
):
    d = lax.axis_index("space")
    i = lax.axis_index("batch")
    h, y = i // 4, i % 4
    y_peers = [(d, h * 4 + (y + o) % 4) for o in (1, 2, 3)]
    z_peer = (d, (1 - h) * 4 + y)
    partners = [(d + (1 - 2 * ((d // s) % 2)) * s, i) for s in (4, 8, 2, 1)]
    blocks = (3, 4, 2, 1)
    everyone = y_peers + [z_peer] + partners
    greet(everyone)

    def load(src, dst, n):
        copy = pltpu.make_async_copy(src, dst, load_sem.at[n])
        copy.start()
        return copy

    row0 = pl.multiple_of(y * ROWS, ROWS)
    prow0 = pl.multiple_of(y * PROWS, PROWS)
    pwin0 = pl.multiple_of((y // 2) * WINDOW, WINDOW)
    mine = [
        load(parent_parts.at[0, pl.ds(pwin0, WINDOW)], own_v.at[pl.ds(0, WINDOW)], 4),
        load(fine_parts.at[0, pl.ds(row0, ROWS)], own_v.at[pl.ds(WINDOW, ROWS)], 5),
    ]
    lists = [
        load(fine_source.at[:, pl.ds(row0, ROWS)], source_v.at[pl.ds(0, NI)], 0),
        load(fine_operator.at[:, pl.ds(row0, ROWS)], kind_v.at[pl.ds(0, NI)], 1),
        load(parent_source.at[pl.ds(prow0, PROWS)], psource_v, 2),
        load(parent_operator.at[pl.ds(prow0, PROWS)], pkind_v, 3),
    ]

    def count_into(source_ref, kind_ref, start, boxes, target):
        for b in range(boxes):
            counted = one_box(
                source_ref[pl.ds(start + b, 1), :], kind_ref[pl.ds(start + b, 1), :], iota_v
            )
            counted_f[0, pl.ds(b, NOPS, stride=boxes + 1), :] = counted[:, :128]
            counted_f[1, pl.ds(b, NOPS, stride=boxes + 1), :] = counted[:, 128:]

        def narrow(step, carry):
            for k in range(8):
                kind = step * 8 + k
                rows = pl.ds(pl.multiple_of(kind * boxes, boxes), boxes)
                wide = pl.ds(kind * (boxes + 1), boxes)
                target[rows, 0:128] = counted_f[0, wide, :].astype(BF16)
                target[rows, 128:256] = counted_f[1, wide, :].astype(BF16)
            return carry

        lax.fori_loop(0, NOPS // 8, narrow, 0)

    def count_windows(first, last):
        def window(w, carry):
            count_into(source_t, kind_t, w * WINDOW, WINDOW, counted_v.at[w])
            return carry

        lax.fori_loop(first, last, window, 0)

    await_greetings(everyone)
    y_copies = []
    for o, device in enumerate(y_peers):
        there = (y + o + 1) % 4
        theirs = pl.multiple_of(there * ROWS, ROWS)
        theirs_p = pl.multiple_of((there // 2) * WINDOW, WINDOW)
        parts = (
            (parent_parts.at[0, pl.ds(theirs_p, WINDOW)], 0, WINDOW),
            (fine_parts.at[0, pl.ds(theirs, FIRST - WINDOW)], WINDOW, FIRST - WINDOW),
            (
                fine_parts.at[0, pl.ds(theirs + FIRST - WINDOW, MESSAGE - FIRST)],
                FIRST,
                MESSAGE - FIRST,
            ),
        )
        y_copies.append(
            [
                remote(
                    src,
                    from_y.at[o, pl.ds(at, rows)],
                    y_send.at[o * 3 + n],
                    y_recv.at[o * 3 + n],
                    device,
                )
                for n, (src, at, rows) in enumerate(parts)
            ]
        )
    for n in range(3):
        for o in (1, 0, 2):
            y_copies[o][n].start()
    weights = [
        load(coarse.at[pl.ds(prow0, PROWS)], coarse_v, 6),
        load(operators, ops_v, 7),
        load(child_shift, shift_v, 8),
        load(basis, basis_v, 9),
    ]
    sends = [copy for copies in y_copies for copy in copies]

    iota_v[...] = lax.broadcasted_iota(jnp.int32, (REACH, 256), 0).astype(F32).astype(BF16)
    for copy in lists:
        copy.wait()
    for lists_v, across in ((psource_v, psource_t), (pkind_v, pkind_t)):
        across[:, 128:256] = jnp.full((PROWS, 128), 255.0, F32)
        across[:, 0:128] = lists_v[:, 0:128].astype(F32)
        across[:, 128:NI] = lists_v[:, 128:NI].astype(F32)
    source_t[...], kind_t[...] = lists_across(source_v, kind_v)
    count_into(psource_t, pkind_t, 0, PROWS, pcounted_v)

    for copy in mine:
        copy.wait()
    z_copies = []
    for n, (part, waits) in enumerate(PIECES):
        for o in range(3):
            for k in waits:
                y_copies[o][k].wait_recv()
        half = own_v[part].astype(F32)
        for o in range(3):
            half = half + from_y[o, part].astype(F32)
        half_v[part] = half.astype(BF16)
        copy = remote(half_v.at[part], from_z.at[part], z_send.at[n], z_recv.at[n], z_peer)
        copy.start()
        z_copies.append(copy)
    sends += z_copies
    count_windows(0, WINDOWS)
    for copy in weights:
        copy.wait()

    n_copies = []
    for n, (part, _) in enumerate(PIECES):
        z_copies[n].wait_recv()
        near_v[0, part] = (half_v[part].astype(F32) + from_z[part].astype(F32)).astype(BF16)
        n_copies.append(
            [
                remote(
                    near_v.at[0, part],
                    near_v.at[block, part],
                    n_send.at[n * 4 + k],
                    n_recv.at[n * 4 + k],
                    device,
                )
                for k, (block, device) in enumerate(zip(blocks, partners))
            ]
        )
        for copy in n_copies[n]:
            copy.start()
        sends += n_copies[n]

    nothing = jnp.zeros((256 - REACH, NC), BF16)
    flat_ops = ops_v[...].reshape(NOPS * NC, NC)
    keep = lax.broadcasted_iota(jnp.int32, (ROWS // 2, NC), 1) < NTERMS
    l_copies = []
    for n, (part, _) in enumerate(PIECES):
        for copy in n_copies[n]:
            copy.wait_recv()
        for w in range(part.start // WINDOW, part.stop // WINDOW):
            boxes = WINDOW if w else PROWS
            at = (w - 1) * WINDOW if w else ROWS
            near = near_v[:, w * WINDOW : (w + 1) * WINDOW, :].reshape(REACH, NC)
            near = jnp.concatenate([near, nothing], axis=0)
            counted = counted_v.at[w - 1] if w else pcounted_v
            kinds = 512 // boxes
            for c in range(NOPS // kinds):
                grouped = jnp.dot(
                    counted[c * 512 : (c + 1) * 512, :], near, preferred_element_type=F32
                ).astype(BF16)
                for t in range(kinds):
                    kind = c * kinds + t
                    grouped_v[at : at + boxes, kind * NC : (kind + 1) * NC] = grouped[
                        t * boxes : (t + 1) * boxes, :
                    ]
        lo = n * (ROWS // 2)
        rows = grouped_v[lo : lo + ROWS // 2, :]
        if n == 0:
            rows = jnp.concatenate([rows, grouped_v[ROWS:, :]], axis=0)
        far = jnp.dot(rows, flat_ops, preferred_element_type=F32)
        if n == 0:
            parent_local = (coarse_v[...] + far[ROWS // 2 :, :]).astype(BF16)
            for octant in range(8):
                spread_v[pl.ds(octant, PROWS, stride=8), :] = jnp.dot(
                    parent_local, shift_v[octant], preferred_element_type=F32
                )
        whole = spread_v[lo : lo + ROWS // 2, :] + far[: ROWS // 2, :]
        here = pl.ds(pl.multiple_of(row0 + lo, ROWS // 2), ROWS // 2)
        local_v[here, :] = jnp.where(keep, whole, 0.0).astype(BF16)
        l_copies.append(
            [
                remote(
                    local_v.at[here], local_v.at[here], l_send.at[n * 3 + o], l_recv.at[n * 3 + o], device
                )
                for o, device in enumerate(y_peers)
            ]
        )
        for o in (1, 0, 2):
            l_copies[n][o].start()
        sends += l_copies[n]

    lane = lax.broadcasted_iota(jnp.int32, (16, ROWS), 1)

    def evaluate(start):
        local = local_v[pl.ds(start, ROWS), :]
        found = jnp.zeros((16, ROWS), F32)
        for c in range(ROWS // 32):
            slots = basis_v[pl.ds(start + c * 32, 32)].reshape(32 * 16, NC)
            values = lax.dot_general(
                slots, local, (((1,), (1,)), ((), ())), preferred_element_type=F32
            )
            for b in range(32):
                found = jnp.where(lane == c * 32 + b, values[b * 16 : (b + 1) * 16, :], found)
        out[:, pl.ds(start, ROWS)] = found

    evaluate(row0)
    for o in (0, 2, 1):
        for n in range(2):
            l_copies[n][o].wait_recv()
        evaluate(pl.multiple_of(((y + 3 - o) % 4) * ROWS, ROWS))
    for copy in sends:
        copy.wait_send()


def body(
    fine_parts,
    parent_parts,
    coarse_local,
    fine_source,
    fine_operator,
    parent_source,
    parent_operator,
    operators,
    child_shift,
    basis,
    counts,
):
    boxes, slots, _ = basis.shape
    vmem = pltpu.VMEM
    dma = pltpu.SemaphoreType.DMA
    values = pl.pallas_call(
        kernel,
        out_shape=jax.ShapeDtypeStruct((slots, boxes), F32),
        in_specs=[pl.BlockSpec(memory_space=pl.ANY)] * 10,
        out_specs=pl.BlockSpec(memory_space=pltpu.VMEM),
        scratch_shapes=[
            vmem((256, ROWS), jnp.int32),
            vmem((256, ROWS), jnp.int32),
            vmem((PROWS, NI), jnp.int32),
            vmem((PROWS, NI), jnp.int32),
            vmem((ROWS, 256), F32),
            vmem((ROWS, 256), F32),
            vmem((PROWS, 256), F32),
            vmem((PROWS, 256), F32),
            vmem((REACH, 256), BF16),
            vmem((MESSAGE, NC), BF16),
            vmem((PROWS, NC), F32),
            vmem((NOPS, NC, NC), BF16),
            vmem((8, NC, NC), BF16),
            vmem((boxes, slots, NC), BF16),
            vmem((2, NOPS * (WINDOW + 1), 128), F32),
            vmem((WINDOWS, NOPS * WINDOW, 256), BF16),
            vmem((NOPS * PROWS, 256), BF16),
            vmem((3, MESSAGE, NC), BF16),
            vmem((MESSAGE, NC), BF16),
            vmem((MESSAGE, NC), BF16),
            vmem((5, MESSAGE, NC), BF16),
            vmem((ROWS + PROWS, NOPS * NC), BF16),
            vmem((ROWS, NC), F32),
            vmem((boxes, NC), BF16),
            dma((10,)),
            dma((9,)),
            dma((9,)),
            dma((2,)),
            dma((2,)),
            dma((8,)),
            dma((8,)),
            dma((6,)),
            dma((6,)),
        ],
        compiler_params=pltpu.CompilerParams(
            collective_id=0, has_side_effects=True, vmem_limit_bytes=61 * 1024 * 1024
        ),
    )(
        fine_parts,
        parent_parts,
        coarse_local,
        fine_source,
        fine_operator,
        parent_source.T,
        parent_operator.T,
        operators,
        child_shift,
        basis,
    )
    slot_index = lax.iota(jnp.int32, slots)[:, None]
    return jnp.where(slot_index < counts, values, 0.0)


def solution(mesh):
    placed = (
        P("batch", "space", None),
        P("batch", "space", None),
        P("space", None),
        P(None, "space"),
        P(None, "space"),
        P(None, "space"),
        P(None, "space"),
        P(),
        P(),
        P("space", "batch", None),
        P("batch", "space"),
    )
    return jax.shard_map(
        body, mesh=mesh, in_specs=placed, out_specs=P("batch", "space"), check_vma=False
    )
```

```python
import functools

import jax
import jax.numpy as jnp
from jax import lax
from jax.experimental import pallas as pl
from jax.experimental.pallas import tpu as pltpu
from jax.sharding import PartitionSpec as P

NTERMS = 121
NI = 189
NC = 128
NOPS = 64
WINDOW = 32
REACH = 5 * WINDOW
ROWS = 128
PROWS = 16
WINDOWS = ROWS // WINDOW
MESSAGE = WINDOW + ROWS
FIRST = 3 * WINDOW
PIECES = ((slice(0, FIRST), (0, 1)), (slice(FIRST, MESSAGE), (2,)))
EARLY = 3
MESH = pl.DeviceIdType.MESH
F32 = jnp.float32
BF16 = jnp.bfloat16


def remote(src, dst, send_sem, recv_sem, device):
    return pltpu.make_async_remote_copy(
        src_ref=src,
        dst_ref=dst,
        send_sem=send_sem,
        recv_sem=recv_sem,
        device_id=device,
        device_id_type=MESH,
    )


def greet(devices):
    barrier = pltpu.get_barrier_semaphore()
    for device in devices:
        pl.semaphore_signal(barrier, inc=1, device_id=device, device_id_type=MESH)


def await_greetings(devices):
    pl.semaphore_wait(pltpu.get_barrier_semaphore(), len(devices))


def one_box(source_row, kind_row, iota_ref):
    source = jnp.broadcast_to(source_row, (16, 256)).astype(BF16)
    kind = jnp.broadcast_to(kind_row, (16, 256)).astype(BF16)
    one, none = jnp.ones((), BF16), jnp.zeros((), BF16)
    iota = iota_ref[...]
    sources = jnp.concatenate([source] * (REACH // 16), axis=0)
    kinds = jnp.concatenate([kind] * (NOPS // 16), axis=0)
    chosen = jnp.where(sources == iota, one, none)
    onehot = jnp.where(kinds == iota[:NOPS], one, none)
    counted = lax.dot_general(
        onehot, chosen, (((1,), (1,)), ((), ())), preferred_element_type=F32
    )
    return jnp.concatenate([counted, jnp.zeros((NOPS, 256 - REACH), F32)], axis=1)


def lists_across(source_v, kind_v):
    entry = lax.broadcasted_iota(jnp.int32, (256, 1), 0)
    source = jnp.where(entry < NI, source_v[...], 255).astype(F32)
    kind = jnp.where(entry < NI, kind_v[...], 255).astype(F32)
    return source.T, kind.T


def kernel(
    fine_parts,
    parent_parts,
    coarse,
    fine_source,
    fine_operator,
    parent_source,
    parent_operator,
    operators,
    child_shift,
    basis,
    counts,
    out,
    source_v,
    kind_v,
    psource_v,
    pkind_v,
    source_t,
    kind_t,
    psource_t,
    pkind_t,
    iota_v,
    own_v,
    coarse_v,
    ops_v,
    shift_v,
    basis_v,
    counted_f,
    counted_v,
    pcounted_v,
    from_y,
    half_v,
    from_z,
    near_v,
    grouped_v,
    spread_v,
    local_v,
    counts_v,
    stage_v,
    pstage_v,
    load_sem,
    y_send,
    y_recv,
    z_send,
    z_recv,
    n_send,
    n_recv,
    l_send,
    l_recv,
):
    d = lax.axis_index("space")
    i = lax.axis_index("batch")
    h, y = i // 4, i % 4
    y_peers = [(d, h * 4 + (y + o) % 4) for o in (1, 2, 3)]
    z_peer = (d, (1 - h) * 4 + y)
    partners = [(d + (1 - 2 * ((d // s) % 2)) * s, i) for s in (4, 8, 2, 1)]
    blocks = (3, 4, 2, 1)
    everyone = y_peers + [z_peer] + partners
    greet(everyone)

    def load(src, dst, n):
        copy = pltpu.make_async_copy(src, dst, load_sem.at[n])
        copy.start()
        return copy

    row0 = pl.multiple_of(y * ROWS, ROWS)
    prow0 = pl.multiple_of(y * PROWS, PROWS)
    pwin0 = pl.multiple_of((y // 2) * WINDOW, WINDOW)
    mine = [
        load(parent_parts.at[0, pl.ds(pwin0, WINDOW)], own_v.at[pl.ds(0, WINDOW)], 4),
        load(fine_parts.at[0, pl.ds(row0, ROWS)], own_v.at[pl.ds(WINDOW, ROWS)], 5),
    ]
    staged = [load(parent_parts.at[0], pstage_v, 10), load(fine_parts.at[0], stage_v, 11)]
    lists = [
        load(fine_source.at[:, pl.ds(row0, ROWS)], source_v.at[pl.ds(0, NI)], 0),
        load(fine_operator.at[:, pl.ds(row0, ROWS)], kind_v.at[pl.ds(0, NI)], 1),
        load(parent_source.at[pl.ds(prow0, PROWS)], psource_v, 2),
        load(parent_operator.at[pl.ds(prow0, PROWS)], pkind_v, 3),
    ]

    def count_into(source_ref, kind_ref, start, boxes, target):
        for b in range(boxes):
            counted = one_box(
                source_ref[pl.ds(start + b, 1), :], kind_ref[pl.ds(start + b, 1), :], iota_v
            )
            counted_f[0, pl.ds(b, NOPS, stride=boxes + 1), :] = counted[:, :128]
            counted_f[1, pl.ds(b, NOPS, stride=boxes + 1), :] = counted[:, 128:]

        def narrow(step, carry):
            for k in range(8):
                kind = step * 8 + k
                rows = pl.ds(pl.multiple_of(kind * boxes, boxes), boxes)
                wide = pl.ds(kind * (boxes + 1), boxes)
                target[rows, 0:128] = counted_f[0, wide, :].astype(BF16)
                target[rows, 128:256] = counted_f[1, wide, :].astype(BF16)
            return carry

        lax.fori_loop(0, NOPS // 8, narrow, 0)

    def count_windows(first, last):
        def window(w, carry):
            count_into(source_t, kind_t, w * WINDOW, WINDOW, counted_v.at[w])
            return carry

        lax.fori_loop(first, last, window, 0)

    def prepare():
        iota_v[...] = lax.broadcasted_iota(jnp.int32, (REACH, 256), 0).astype(F32).astype(BF16)
        for copy in lists:
            copy.wait()
        for lists_v, across in ((psource_v, psource_t), (pkind_v, pkind_t)):
            across[:, 128:256] = jnp.full((PROWS, 128), 255.0, F32)
            across[:, 0:128] = lists_v[:, 0:128].astype(F32)
            across[:, 128:NI] = lists_v[:, 128:NI].astype(F32)
        source_t[...], kind_t[...] = lists_across(source_v, kind_v)
        count_into(psource_t, pkind_t, 0, PROWS, pcounted_v)

    @pl.when(h == 0)
    def _():
        prepare()
        count_windows(0, EARLY)

    await_greetings(everyone)
    for copy in staged:
        copy.wait()
    y_copies = []
    for o, device in enumerate(y_peers):
        there = (y + o + 1) % 4
        theirs = pl.multiple_of(there * ROWS, ROWS)
        theirs_p = pl.multiple_of((there // 2) * WINDOW, WINDOW)
        parts = (
            (pstage_v.at[pl.ds(theirs_p, WINDOW)], 0, WINDOW),
            (stage_v.at[pl.ds(theirs, FIRST - WINDOW)], WINDOW, FIRST - WINDOW),
            (
                stage_v.at[pl.ds(theirs + FIRST - WINDOW, MESSAGE - FIRST)],
                FIRST,
                MESSAGE - FIRST,
            ),
        )
        y_copies.append(
            [
                remote(
                    src,
                    from_y.at[o, pl.ds(at, rows)],
                    y_send.at[o * 3 + n],
                    y_recv.at[o * 3 + n],
                    device,
                )
                for n, (src, at, rows) in enumerate(parts)
            ]
        )
    for n in range(3):
        for o in (1, 0, 2):
            y_copies[o][n].start()
    weights = [
        load(coarse.at[pl.ds(prow0, PROWS)], coarse_v, 6),
        load(operators, ops_v, 7),
        load(child_shift, shift_v, 8),
        load(basis, basis_v, 9),
        load(counts, counts_v, 12),
    ]
    sends = [copy for copies in y_copies for copy in copies]

    pl.when(h == 1)(prepare)

    for copy in mine:
        copy.wait()
    z_copies = []
    for n, (part, waits) in enumerate(PIECES):
        for o in range(3):
            for k in waits:
                y_copies[o][k].wait_recv()
        half = own_v[part].astype(F32)
        for o in range(3):
            half = half + from_y[o, part].astype(F32)
        half_v[part] = half.astype(BF16)
        copy = remote(half_v.at[part], from_z.at[part], z_send.at[n], z_recv.at[n], z_peer)
        copy.start()
        z_copies.append(copy)
    sends += z_copies
    count_windows(jnp.where(h == 0, EARLY, 0), WINDOWS)
    for copy in weights:
        copy.wait()

    n_copies = []
    for n, (part, _) in enumerate(PIECES):
        z_copies[n].wait_recv()
        near_v[0, part] = (half_v[part].astype(F32) + from_z[part].astype(F32)).astype(BF16)
        n_copies.append(
            [
                remote(
                    near_v.at[0, part],
                    near_v.at[block, part],
                    n_send.at[n * 4 + k],
                    n_recv.at[n * 4 + k],
                    device,
                )
                for k, (block, device) in enumerate(zip(blocks, partners))
            ]
        )
        for copy in n_copies[n]:
            copy.start()
        sends += n_copies[n]

    nothing = jnp.zeros((256 - REACH, NC), BF16)
    flat_ops = ops_v[...].reshape(NOPS * NC, NC)
    keep = lax.broadcasted_iota(jnp.int32, (ROWS // 2, NC), 1) < NTERMS
    l_copies = []
    for n, (part, _) in enumerate(PIECES):
        for copy in n_copies[n]:
            copy.wait_recv()
        for w in range(part.start // WINDOW, part.stop // WINDOW):
            boxes = WINDOW if w else PROWS
            at = (w - 1) * WINDOW if w else ROWS
            near = near_v[:, w * WINDOW : (w + 1) * WINDOW, :].reshape(REACH, NC)
            near = jnp.concatenate([near, nothing], axis=0)
            counted = counted_v.at[w - 1] if w else pcounted_v
            kinds = 512 // boxes
            for c in range(NOPS // kinds):
                grouped = jnp.dot(
                    counted[c * 512 : (c + 1) * 512, :], near, preferred_element_type=F32
                ).astype(BF16)
                for t in range(kinds):
                    kind = c * kinds + t
                    grouped_v[at : at + boxes, kind * NC : (kind + 1) * NC] = grouped[
                        t * boxes : (t + 1) * boxes, :
                    ]
        lo = n * (ROWS // 2)
        rows = grouped_v[lo : lo + ROWS // 2, :]
        if n == 0:
            rows = jnp.concatenate([rows, grouped_v[ROWS:, :]], axis=0)
        far = jnp.dot(rows, flat_ops, preferred_element_type=F32)
        if n == 0:
            parent_local = (coarse_v[...] + far[ROWS // 2 :, :]).astype(BF16)
            for octant in range(8):
                spread_v[pl.ds(octant, PROWS, stride=8), :] = jnp.dot(
                    parent_local, shift_v[octant], preferred_element_type=F32
                )
        whole = spread_v[lo : lo + ROWS // 2, :] + far[: ROWS // 2, :]
        here = pl.ds(pl.multiple_of(row0 + lo, ROWS // 2), ROWS // 2)
        local_v[here, :] = jnp.where(keep, whole, 0.0).astype(BF16)
        l_copies.append(
            [
                remote(
                    local_v.at[here], local_v.at[here], l_send.at[n * 3 + o], l_recv.at[n * 3 + o], device
                )
                for o, device in enumerate(y_peers)
            ]
        )
        for o in (1, 0, 2):
            l_copies[n][o].start()
        sends += l_copies[n]

    lane = lax.broadcasted_iota(jnp.int32, (16, ROWS), 1)

    def evaluate(start):
        local = local_v[pl.ds(start, ROWS), :]
        found = jnp.zeros((16, ROWS), F32)
        for c in range(ROWS // 32):
            slots = basis_v[pl.ds(start + c * 32, 32)].reshape(32 * 16, NC)
            values = lax.dot_general(
                slots, local, (((1,), (1,)), ((), ())), preferred_element_type=F32
            )
            for b in range(32):
                found = jnp.where(lane == c * 32 + b, values[b * 16 : (b + 1) * 16, :], found)
        slot = lax.broadcasted_iota(jnp.int32, (16, ROWS), 0)
        out[:, pl.ds(start, ROWS)] = jnp.where(slot < counts_v[:, pl.ds(start, ROWS)], found, 0.0)

    evaluate(row0)
    for o in (0, 2, 1):
        for n in range(2):
            l_copies[n][o].wait_recv()
        evaluate(pl.multiple_of(((y + 3 - o) % 4) * ROWS, ROWS))
    for copy in sends:
        copy.wait_send()


def body(
    fine_parts,
    parent_parts,
    coarse_local,
    fine_source,
    fine_operator,
    parent_source,
    parent_operator,
    operators,
    child_shift,
    basis,
    counts,
):
    boxes, slots, _ = basis.shape
    vmem = pltpu.VMEM
    dma = pltpu.SemaphoreType.DMA
    return pl.pallas_call(
        kernel,
        out_shape=jax.ShapeDtypeStruct((slots, boxes), F32),
        in_specs=[pl.BlockSpec(memory_space=pl.ANY)] * 11,
        out_specs=pl.BlockSpec(memory_space=pltpu.VMEM),
        scratch_shapes=[
            vmem((256, ROWS), jnp.int32),
            vmem((256, ROWS), jnp.int32),
            vmem((PROWS, NI), jnp.int32),
            vmem((PROWS, NI), jnp.int32),
            vmem((ROWS, 256), F32),
            vmem((ROWS, 256), F32),
            vmem((PROWS, 256), F32),
            vmem((PROWS, 256), F32),
            vmem((REACH, 256), BF16),
            vmem((MESSAGE, NC), BF16),
            vmem((PROWS, NC), F32),
            vmem((NOPS, NC, NC), BF16),
            vmem((8, NC, NC), BF16),
            vmem((boxes, slots, NC), BF16),
            vmem((2, NOPS * (WINDOW + 1), 128), F32),
            vmem((WINDOWS, NOPS * WINDOW, 256), BF16),
            vmem((NOPS * PROWS, 256), BF16),
            vmem((3, MESSAGE, NC), BF16),
            vmem((MESSAGE, NC), BF16),
            vmem((MESSAGE, NC), BF16),
            vmem((5, MESSAGE, NC), BF16),
            vmem((ROWS + PROWS, NOPS * NC), BF16),
            vmem((ROWS, NC), F32),
            vmem((boxes, NC), BF16),
            vmem((1, boxes), jnp.int32),
            vmem((boxes, NC), BF16),
            vmem((64, NC), BF16),
            dma((13,)),
            dma((9,)),
            dma((9,)),
            dma((2,)),
            dma((2,)),
            dma((8,)),
            dma((8,)),
            dma((6,)),
            dma((6,)),
        ],
        compiler_params=pltpu.CompilerParams(
            collective_id=0, has_side_effects=True, vmem_limit_bytes=61 * 1024 * 1024
        ),
    )(
        fine_parts,
        parent_parts,
        coarse_local,
        fine_source,
        fine_operator,
        parent_source.T,
        parent_operator.T,
        operators,
        child_shift,
        basis,
        counts,
    )


def solution(mesh):
    placed = (
        P("batch", "space", None),
        P("batch", "space", None),
        P("space", None),
        P(None, "space"),
        P(None, "space"),
        P(None, "space"),
        P(None, "space"),
        P(),
        P(),
        P("space", "batch", None),
        P("batch", "space"),
    )
    return jax.shard_map(
        body, mesh=mesh, in_specs=placed, out_specs=P("batch", "space"), check_vma=False
    )
```

```python
import functools

import jax
import jax.numpy as jnp
from jax import lax
from jax.experimental import pallas as pl
from jax.experimental.pallas import tpu as pltpu
from jax.sharding import PartitionSpec as P

NTERMS = 121
NI = 189
NC = 128
NOPS = 64
WINDOW = 32
REACH = 5 * WINDOW
ROWS = 128
PROWS = 16
WINDOWS = ROWS // WINDOW
MESSAGE = WINDOW + ROWS
FIRST = 3 * WINDOW
PIECES = ((slice(0, FIRST), (0, 1)), (slice(FIRST, MESSAGE), (2,)))
EARLY = 3
MESH = pl.DeviceIdType.MESH
F32 = jnp.float32
BF16 = jnp.bfloat16


def remote(src, dst, send_sem, recv_sem, device):
    return pltpu.make_async_remote_copy(
        src_ref=src,
        dst_ref=dst,
        send_sem=send_sem,
        recv_sem=recv_sem,
        device_id=device,
        device_id_type=MESH,
    )


def greet(devices):
    barrier = pltpu.get_barrier_semaphore()
    for device in devices:
        pl.semaphore_signal(barrier, inc=1, device_id=device, device_id_type=MESH)


def await_greetings(devices):
    pl.semaphore_wait(pltpu.get_barrier_semaphore(), len(devices))


def one_box(source_row, kind_row, iota_ref):
    source = jnp.broadcast_to(source_row, (16, 256)).astype(BF16)
    kind = jnp.broadcast_to(kind_row, (16, 256)).astype(BF16)
    one, none = jnp.ones((), BF16), jnp.zeros((), BF16)
    iota = iota_ref[...]
    sources = jnp.concatenate([source] * (REACH // 16), axis=0)
    kinds = jnp.concatenate([kind] * (NOPS // 16), axis=0)
    chosen = jnp.where(sources == iota, one, none)
    onehot = jnp.where(kinds == iota[:NOPS], one, none)
    counted = lax.dot_general(
        onehot, chosen, (((1,), (1,)), ((), ())), preferred_element_type=F32
    )
    return jnp.concatenate([counted, jnp.zeros((NOPS, 256 - REACH), F32)], axis=1)


def lists_across(source_v, kind_v):
    entry = lax.broadcasted_iota(jnp.int32, (256, 1), 0)
    source = jnp.where(entry < NI, source_v[...], 255).astype(F32)
    kind = jnp.where(entry < NI, kind_v[...], 255).astype(F32)
    return source.T, kind.T


def kernel(
    fine_parts,
    parent_parts,
    coarse,
    fine_source,
    fine_operator,
    parent_source,
    parent_operator,
    operators,
    child_shift,
    basis,
    counts,
    out,
    source_v,
    kind_v,
    psource_v,
    pkind_v,
    source_t,
    kind_t,
    psource_t,
    pkind_t,
    iota_v,
    own_v,
    coarse_v,
    ops_v,
    shift_v,
    basis_v,
    counted_f,
    counted_v,
    pcounted_v,
    from_y,
    half_v,
    from_z,
    near_v,
    grouped_v,
    spread_v,
    local_v,
    counts_v,
    stage_v,
    pstage_v,
    load_sem,
    y_send,
    y_recv,
    z_send,
    z_recv,
    n_send,
    n_recv,
    l_send,
    l_recv,
):
    d = lax.axis_index("space")
    i = lax.axis_index("batch")
    h, y = i // 4, i % 4
    y_peers = [(d, h * 4 + (y + o) % 4) for o in (1, 2, 3)]
    z_peer = (d, (1 - h) * 4 + y)
    partners = [(d + (1 - 2 * ((d // s) % 2)) * s, i) for s in (4, 8, 2, 1)]
    blocks = (3, 4, 2, 1)
    everyone = y_peers + [z_peer] + partners
    greet(everyone)

    def load(src, dst, n):
        copy = pltpu.make_async_copy(src, dst, load_sem.at[n])
        copy.start()
        return copy

    row0 = pl.multiple_of(y * ROWS, ROWS)
    prow0 = pl.multiple_of(y * PROWS, PROWS)
    pwin0 = pl.multiple_of((y // 2) * WINDOW, WINDOW)
    mine = [
        load(parent_parts.at[0, pl.ds(pwin0, WINDOW)], own_v.at[pl.ds(0, WINDOW)], 4),
        load(fine_parts.at[0, pl.ds(row0, ROWS)], own_v.at[pl.ds(WINDOW, ROWS)], 5),
    ]
    staged = [load(parent_parts.at[0], pstage_v, 10), load(fine_parts.at[0], stage_v, 11)]
    lists = [
        load(fine_source.at[:, pl.ds(row0, ROWS)], source_v.at[pl.ds(0, NI)], 0),
        load(fine_operator.at[:, pl.ds(row0, ROWS)], kind_v.at[pl.ds(0, NI)], 1),
        load(parent_source.at[pl.ds(prow0, PROWS)], psource_v, 2),
        load(parent_operator.at[pl.ds(prow0, PROWS)], pkind_v, 3),
    ]

    def count_into(source_ref, kind_ref, start, boxes, target):
        for b in range(boxes):
            counted = one_box(
                source_ref[pl.ds(start + b, 1), :], kind_ref[pl.ds(start + b, 1), :], iota_v
            )
            counted_f[0, pl.ds(b, NOPS, stride=boxes + 1), :] = counted[:, :128]
            counted_f[1, pl.ds(b, NOPS, stride=boxes + 1), :] = counted[:, 128:]

        def narrow(step, carry):
            for k in range(8):
                kind = step * 8 + k
                rows = pl.ds(pl.multiple_of(kind * boxes, boxes), boxes)
                wide = pl.ds(kind * (boxes + 1), boxes)
                target[rows, 0:128] = counted_f[0, wide, :].astype(BF16)
                target[rows, 128:256] = counted_f[1, wide, :].astype(BF16)
            return carry

        lax.fori_loop(0, NOPS // 8, narrow, 0)

    def count_windows(first, last):
        def window(w, carry):
            count_into(source_t, kind_t, w * WINDOW, WINDOW, counted_v.at[w])
            return carry

        lax.fori_loop(first, last, window, 0)

    def count_parents():
        count_into(psource_t, pkind_t, 0, PROWS, pcounted_v)

    def prepare():
        iota_v[...] = lax.broadcasted_iota(jnp.int32, (REACH, 256), 0).astype(F32).astype(BF16)
        for copy in lists:
            copy.wait()
        for lists_v, across in ((psource_v, psource_t), (pkind_v, pkind_t)):
            across[:, 128:256] = jnp.full((PROWS, 128), 255.0, F32)
            across[:, 0:128] = lists_v[:, 0:128].astype(F32)
            across[:, 128:NI] = lists_v[:, 128:NI].astype(F32)
        source_t[...], kind_t[...] = lists_across(source_v, kind_v)

    @pl.when(h == 0)
    def _():
        prepare()
        count_parents()
        count_windows(0, EARLY)

    await_greetings(everyone)
    for copy in staged:
        copy.wait()
    y_copies = []
    for o, device in enumerate(y_peers):
        there = (y + o + 1) % 4
        theirs = pl.multiple_of(there * ROWS, ROWS)
        theirs_p = pl.multiple_of((there // 2) * WINDOW, WINDOW)
        parts = (
            (pstage_v.at[pl.ds(theirs_p, WINDOW)], 0, WINDOW),
            (stage_v.at[pl.ds(theirs, FIRST - WINDOW)], WINDOW, FIRST - WINDOW),
            (
                stage_v.at[pl.ds(theirs + FIRST - WINDOW, MESSAGE - FIRST)],
                FIRST,
                MESSAGE - FIRST,
            ),
        )
        y_copies.append(
            [
                remote(
                    src,
                    from_y.at[o, pl.ds(at, rows)],
                    y_send.at[o * 3 + n],
                    y_recv.at[o * 3 + n],
                    device,
                )
                for n, (src, at, rows) in enumerate(parts)
            ]
        )
    for n in range(3):
        for o in (1, 0, 2):
            y_copies[o][n].start()
    sends = [copy for copies in y_copies for copy in copies]

    pl.when(h == 1)(prepare)

    for copy in mine:
        copy.wait()
    z_copies = []
    for n, (part, waits) in enumerate(PIECES):
        for o in range(3):
            for k in waits:
                y_copies[o][k].wait_recv()
        half = own_v[part].astype(F32)
        for o in range(3):
            half = half + from_y[o, part].astype(F32)
        half_v[part] = half.astype(BF16)
        copy = remote(half_v.at[part], from_z.at[part], z_send.at[n], z_recv.at[n], z_peer)
        copy.start()
        z_copies.append(copy)
    sends += z_copies
    weights = [
        load(coarse.at[pl.ds(prow0, PROWS)], coarse_v, 6),
        load(operators, ops_v, 7),
        load(child_shift, shift_v, 8),
        load(basis, basis_v, 9),
        load(counts, counts_v, 12),
    ]
    pl.when(h == 1)(count_parents)
    count_windows(jnp.where(h == 0, EARLY, 0), WINDOWS)
    for copy in weights:
        copy.wait()

    n_copies = []
    for n, (part, _) in enumerate(PIECES):
        z_copies[n].wait_recv()
        near_v[0, part] = (half_v[part].astype(F32) + from_z[part].astype(F32)).astype(BF16)
        n_copies.append(
            [
                remote(
                    near_v.at[0, part],
                    near_v.at[block, part],
                    n_send.at[n * 4 + k],
                    n_recv.at[n * 4 + k],
                    device,
                )
                for k, (block, device) in enumerate(zip(blocks, partners))
            ]
        )
        for copy in n_copies[n]:
            copy.start()
        sends += n_copies[n]

    nothing = jnp.zeros((256 - REACH, NC), BF16)
    flat_ops = ops_v[...].reshape(NOPS * NC, NC)
    keep = lax.broadcasted_iota(jnp.int32, (ROWS // 2, NC), 1) < NTERMS
    l_copies = []
    for n, (part, _) in enumerate(PIECES):
        for copy in n_copies[n]:
            copy.wait_recv()
        for w in range(part.start // WINDOW, part.stop // WINDOW):
            boxes = WINDOW if w else PROWS
            at = (w - 1) * WINDOW if w else ROWS
            near = near_v[:, w * WINDOW : (w + 1) * WINDOW, :].reshape(REACH, NC)
            near = jnp.concatenate([near, nothing], axis=0)
            counted = counted_v.at[w - 1] if w else pcounted_v
            kinds = 512 // boxes
            for c in range(NOPS // kinds):
                grouped = jnp.dot(
                    counted[c * 512 : (c + 1) * 512, :], near, preferred_element_type=F32
                ).astype(BF16)
                for t in range(kinds):
                    kind = c * kinds + t
                    grouped_v[at : at + boxes, kind * NC : (kind + 1) * NC] = grouped[
                        t * boxes : (t + 1) * boxes, :
                    ]
        lo = n * (ROWS // 2)
        rows = grouped_v[lo : lo + ROWS // 2, :]
        if n == 0:
            rows = jnp.concatenate([rows, grouped_v[ROWS:, :]], axis=0)
        far = jnp.dot(rows, flat_ops, preferred_element_type=F32)
        if n == 0:
            parent_local = (coarse_v[...] + far[ROWS // 2 :, :]).astype(BF16)
            for octant in range(8):
                spread_v[pl.ds(octant, PROWS, stride=8), :] = jnp.dot(
                    parent_local, shift_v[octant], preferred_element_type=F32
                )
        whole = spread_v[lo : lo + ROWS // 2, :] + far[: ROWS // 2, :]
        here = pl.ds(pl.multiple_of(row0 + lo, ROWS // 2), ROWS // 2)
        local_v[here, :] = jnp.where(keep, whole, 0.0).astype(BF16)
        l_copies.append(
            [
                remote(
                    local_v.at[here], local_v.at[here], l_send.at[n * 3 + o], l_recv.at[n * 3 + o], device
                )
                for o, device in enumerate(y_peers)
            ]
        )
        for o in (1, 0, 2):
            l_copies[n][o].start()
        sends += l_copies[n]

    lane = lax.broadcasted_iota(jnp.int32, (16, ROWS), 1)

    def evaluate(start):
        local = local_v[pl.ds(start, ROWS), :]
        found = jnp.zeros((16, ROWS), F32)
        for c in range(ROWS // 32):
            slots = basis_v[pl.ds(start + c * 32, 32)].reshape(32 * 16, NC)
            values = lax.dot_general(
                slots, local, (((1,), (1,)), ((), ())), preferred_element_type=F32
            )
            for b in range(32):
                found = jnp.where(lane == c * 32 + b, values[b * 16 : (b + 1) * 16, :], found)
        slot = lax.broadcasted_iota(jnp.int32, (16, ROWS), 0)
        out[:, pl.ds(start, ROWS)] = jnp.where(slot < counts_v[:, pl.ds(start, ROWS)], found, 0.0)

    evaluate(row0)
    for o in (0, 2, 1):
        for n in range(2):
            l_copies[n][o].wait_recv()
        evaluate(pl.multiple_of(((y + 3 - o) % 4) * ROWS, ROWS))
    for copy in sends:
        copy.wait_send()


def body(
    fine_parts,
    parent_parts,
    coarse_local,
    fine_source,
    fine_operator,
    parent_source,
    parent_operator,
    operators,
    child_shift,
    basis,
    counts,
):
    boxes, slots, _ = basis.shape
    vmem = pltpu.VMEM
    dma = pltpu.SemaphoreType.DMA
    return pl.pallas_call(
        kernel,
        out_shape=jax.ShapeDtypeStruct((slots, boxes), F32),
        in_specs=[pl.BlockSpec(memory_space=pl.ANY)] * 11,
        out_specs=pl.BlockSpec(memory_space=pltpu.VMEM),
        scratch_shapes=[
            vmem((256, ROWS), jnp.int32),
            vmem((256, ROWS), jnp.int32),
            vmem((PROWS, NI), jnp.int32),
            vmem((PROWS, NI), jnp.int32),
            vmem((ROWS, 256), F32),
            vmem((ROWS, 256), F32),
            vmem((PROWS, 256), F32),
            vmem((PROWS, 256), F32),
            vmem((REACH, 256), BF16),
            vmem((MESSAGE, NC), BF16),
            vmem((PROWS, NC), F32),
            vmem((NOPS, NC, NC), BF16),
            vmem((8, NC, NC), BF16),
            vmem((boxes, slots, NC), BF16),
            vmem((2, NOPS * (WINDOW + 1), 128), F32),
            vmem((WINDOWS, NOPS * WINDOW, 256), BF16),
            vmem((NOPS * PROWS, 256), BF16),
            vmem((3, MESSAGE, NC), BF16),
            vmem((MESSAGE, NC), BF16),
            vmem((MESSAGE, NC), BF16),
            vmem((5, MESSAGE, NC), BF16),
            vmem((ROWS + PROWS, NOPS * NC), BF16),
            vmem((ROWS, NC), F32),
            vmem((boxes, NC), BF16),
            vmem((1, boxes), jnp.int32),
            vmem((boxes, NC), BF16),
            vmem((64, NC), BF16),
            dma((13,)),
            dma((9,)),
            dma((9,)),
            dma((2,)),
            dma((2,)),
            dma((8,)),
            dma((8,)),
            dma((6,)),
            dma((6,)),
        ],
        compiler_params=pltpu.CompilerParams(
            collective_id=0, has_side_effects=True, vmem_limit_bytes=61 * 1024 * 1024
        ),
    )(
        fine_parts,
        parent_parts,
        coarse_local,
        fine_source,
        fine_operator,
        parent_source.T,
        parent_operator.T,
        operators,
        child_shift,
        basis,
        counts,
    )


def solution(mesh):
    placed = (
        P("batch", "space", None),
        P("batch", "space", None),
        P("space", None),
        P(None, "space"),
        P(None, "space"),
        P(None, "space"),
        P(None, "space"),
        P(),
        P(),
        P("space", "batch", None),
        P("batch", "space"),
    )
    return jax.shard_map(
        body, mesh=mesh, in_specs=placed, out_specs=P("batch", "space"), check_vma=False
    )
```
